128 devices in a mesh: roll: 8 (over y, core), seq: 16 (over z, x).
Axes of the slice: x: 4, y: 4, z: 4, core: 2. Of those that a mesh axis runs over, the one named last changes fastest.
Arguments:
- queries: bfloat16 [8, 4, 128, 192], P('roll', None, 'seq'), may hold values from -17 to 17
- latent_cache: bfloat16 [8, 131072, 576], P('roll', 'seq'), may hold values from -6 to 6
- lengths: int32 [8], P('roll'), may hold values from 8192 to 131072, as said below
- key_weight: bfloat16 [128, 128, 512], P('seq', None, 'roll'), may hold values from -0.5 to 0.5
- value_weight: bfloat16 [128, 512, 128], P('seq', 'roll'), may hold values from -1.5 to 1.5
Outputs:
- attended: bfloat16 [8, 4, 128, 128], P('roll', None, 'seq')
The draws below stay inside these ranges and needn't reach their ends.
Inputs may be any that keep to these rules, and one draw needn't show every extreme that they name: `lengths`: at least 8192; some rollout has all 131072 positions live.
All inputs are finite; a program needn't handle non-finite values.
Results may differ from the reference program's by a relative error of at most 0.0068.
Values may be sent and summed in bfloat16 or wider, within the bound.
No kernel may reach another device: no remote copies, remote signals or barrier semaphores. Data moves between devices by JAX's collectives and lax.ppermute only.
A program may use at most 128 MiB of HBM per device.

```python
import jax
import jax.numpy as jnp
from jax import lax

HEADS = 128
NOPE = 128
ROPE = 64
LATENT = 512
VHEAD = 128
FRAMES = 4
CT_DEV = 8192
ROLLOUTS = 8
CACHE = 131072


def shared_lengths(key):
    length_key = jax.random.fold_in(key, 103)
    key_len, key_full = jax.random.split(length_key)
    drawn = jax.random.randint(key_len, (ROLLOUTS,), CT_DEV, CACHE + 1)
    longest = jax.random.randint(key_full, (), 0, ROLLOUTS)
    return jnp.where(jnp.arange(ROLLOUTS) == longest, CACHE, drawn).astype(jnp.int32)


def draw_latent_cache(key, part):
    key = jax.random.fold_in(key, 1)
    draw_shape = (ROLLOUTS, CACHE, LATENT + ROPE)
    sample = jnp.clip(jax.random.normal(key, draw_shape), -6.0, 6.0)
    return sample.astype(jnp.bfloat16)


def draw_queries(key, part):
    key = jax.random.fold_in(key, 2)
    key_base = jax.random.fold_in(key, 0)
    draw_shape = (ROLLOUTS, FRAMES, HEADS, NOPE + ROPE)
    sample = jnp.clip(1.5 * jax.random.normal(key_base, draw_shape), -9.0, 9.0)
    return sample.astype(jnp.bfloat16)


def draw_lengths(key, part):
    return shared_lengths(key)


def steps_of(rng, dims, shards, least, top_value):
    loudness, own = 1.0, jax.random.fold_in(rng, 6)
    for axis_at, blocks in shards:
        draws = jnp.exp(jax.random.uniform(jax.random.fold_in(own, axis_at), (blocks,), jnp.float32, least / len(shards), top_value / len(shards)))
        loudness = loudness * jnp.repeat(draws, dims[axis_at] // blocks).reshape([-1 if axis == axis_at else 1 for axis in range(len(dims))])
    return loudness


def gaussian(own_key, extent, spread, limit, pieces=(), held_as=jnp.bfloat16):
    array = spread * jax.random.normal(own_key, extent, jnp.float32)
    if pieces:
        array = array * steps_of(own_key, extent, pieces, -0.22, 0.18)
    return jnp.clip(array, -limit, limit).astype(held_as)


def setup_inputs(seed: int = 0) -> dict:
    keys = jax.random.split(jax.random.key(seed), 6)
    queries = draw_queries(jax.random.fold_in(keys[5], 71), 0)
    latent_cache = draw_latent_cache(jax.random.fold_in(keys[5], 71), 0)
    lengths = draw_lengths(jax.random.fold_in(keys[5], 71), 0)
    key_weight = gaussian(keys[3], (HEADS, NOPE, LATENT), NOPE ** -0.5, 0.5, ((0, 16), (2, 8)))
    value_weight = gaussian(keys[4], (HEADS, LATENT, VHEAD), (LATENT // 32) ** -0.5, 1.5, ((0, 16), (1, 8)))
    return dict(queries=queries, latent_cache=latent_cache, lengths=lengths, key_weight=key_weight, value_weight=value_weight)


masked_value = -1e30


def block_partials(query_rows, key_block, positions, live_length, softmax_scale):
    scores = jnp.dot(query_rows, key_block.T, preferred_element_type=jnp.float32) * softmax_scale
    live_mask = positions[None, :] < live_length
    masked = jnp.where(live_mask, scores, masked_value)
    row_top = jnp.max(masked, axis=1)
    weights = jnp.where(live_mask, jnp.exp(masked - row_top[:, None]), 0.0)
    row_total = jnp.sum(weights, axis=1)
    block_out = jnp.dot(weights.astype(jnp.bfloat16), key_block[:, :LATENT], preferred_element_type=jnp.float32)
    return block_out, row_top, row_total


def reference(queries, latent_cache, lengths, key_weight, value_weight):
    softmax_scale = (NOPE + ROPE) ** -0.5
    absorbed = jnp.einsum("bthn,hnl->bthl", queries[..., :NOPE].astype(jnp.float32),
                          key_weight.astype(jnp.float32)).astype(jnp.bfloat16)
    full_query = jnp.concatenate([absorbed, queries[..., NOPE:]], axis=-1)
    block_size = min(2048, CT_DEV)
    block_count = CACHE // block_size

    def one_rollout(packed):
        query_block, cache_rows, live_length = packed
        query_rows = query_block.reshape(FRAMES * HEADS, LATENT + ROPE)

        def one_block(block_index):
            key_block = lax.dynamic_slice_in_dim(cache_rows, block_index * block_size, block_size, 0)
            positions = block_index * block_size + jnp.arange(block_size, dtype=jnp.int32)
            return block_partials(query_rows, key_block, positions, live_length, softmax_scale)

        block_outs, block_tops, totals = lax.map(one_block, jnp.arange(block_count, dtype=jnp.int32))
        summit = jnp.max(block_tops, axis=0)
        factor = jnp.exp(block_tops - summit[None, :])
        merged = jnp.sum(block_outs * factor[:, :, None], axis=0)
        denominator = jnp.sum(totals * factor, axis=0)
        return (merged / denominator[:, None]).reshape(FRAMES, HEADS, LATENT)

    context = lax.map(one_rollout, (full_query, latent_cache, lengths)).astype(jnp.bfloat16)
    result = jnp.einsum("bthl,hlv->bthv", context.astype(jnp.float32), value_weight.astype(jnp.float32))
    return result.astype(jnp.bfloat16)
```

```python
import functools

import jax
import jax.numpy as jnp
from jax import lax
from jax.experimental import pallas as pl
from jax.experimental.pallas import tpu as pltpu
from jax.sharding import PartitionSpec as P

NOPE = 128
ROPE = 64
LATENT = 512
WIDTH = LATENT + ROPE
PAYLOAD = LATENT + 128
RING = 4
CORES = 2

MASKED = -1e30
TO_LOG2 = (NOPE + ROPE) ** (-0.5) * 1.4426950408889634

VMEM = pl.BlockSpec(memory_space=pltpu.VMEM)
SMEM = pl.BlockSpec(memory_space=pltpu.SMEM)
ANY = pl.BlockSpec(memory_space=pl.ANY)
BF16 = jnp.bfloat16
F32 = jnp.float32


def y_shift(value, hops):
    pairs = [(CORES * y + c, CORES * ((y + hops) % RING) + c) for y in range(RING) for c in range(CORES)]
    return lax.ppermute(value, "roll", pairs)


def core_swap(value):
    pairs = [(CORES * y + c, CORES * y + 1 - c) for y in range(RING) for c in range(CORES)]
    return lax.ppermute(value, "roll", pairs)


def z_shift(value, hops):
    pairs = [(RING * z + x, RING * ((z + hops) % RING) + x) for z in range(RING) for x in range(RING)]
    return lax.ppermute(value, "seq", pairs)


def x_shift(value, hops):
    pairs = [(RING * z + x, RING * z + (x + hops) % RING) for z in range(RING) for x in range(RING)]
    return lax.ppermute(value, "seq", pairs)


def two_terms(value):
    high = value.astype(BF16).astype(F32)
    return high, (value - high).astype(BF16).astype(F32)


def pack_stats(top, total, rows):
    lane = lax.broadcasted_iota(jnp.int32, (rows, 128), 1)
    packed = jnp.zeros((rows, 128), F32)
    for at, term in enumerate(two_terms(top) + two_terms(total)):
        packed = jnp.where(lane == at, term, packed)
    return packed.astype(BF16)


def merge(parts):
    tops, totals = [], []
    for part in parts:
        stats = part[:, LATENT:].astype(F32)
        tops.append(stats[:, 0:1] + stats[:, 1:2])
        totals.append(stats[:, 2:3] + stats[:, 3:4])
    top = functools.reduce(jnp.maximum, tops)
    weights = [jnp.exp2(t - top) * n for t, n in zip(tops, totals)]
    total = functools.reduce(jnp.add, weights)
    inverse = jnp.where(total > 0, 1.0 / total, 0.0)
    out = functools.reduce(
        jnp.add, [part[:, :LATENT].astype(F32) * (w * inverse) for part, w in zip(parts, weights)]
    )
    return out, top, total


def absorb_kernel(place, mine, other, kw0, kw1, kw2, kw3, out_mine, out_other, weights):
    y, core = place[0], place[1]
    heads = mine.shape[1]
    weights[...] = jnp.zeros_like(weights)
    for hops, block in enumerate((kw0, kw1, kw2, kw3)):
        chunk = lax.rem(y + RING - hops, RING) * CORES + core
        weights[:, pl.ds(pl.multiple_of(chunk * 64, 64), 64), :] = block[...]
    for h in range(heads):
        rows = jnp.concatenate([mine[:, h, :], other[:, h, :]], axis=0)
        absorbed = lax.dot_general(
            rows[:, :NOPE], weights[h], (((1,), (1,)), ((), ())), preferred_element_type=F32
        ).astype(BF16)
        out_mine[h] = jnp.concatenate([absorbed[:4], rows[:4, NOPE:]], axis=1)
        out_other[h] = jnp.concatenate([absorbed[4:], jnp.zeros((4, ROPE), BF16)], axis=1)


def absorb(place, mine, other, blocks):
    frames, heads, _ = mine.shape
    shape = jax.ShapeDtypeStruct((heads, frames, WIDTH), BF16)
    return pl.pallas_call(
        absorb_kernel,
        out_shape=[shape, shape],
        in_specs=[SMEM] + [VMEM] * 6,
        out_specs=[VMEM, VMEM],
        scratch_shapes=[pltpu.VMEM((heads, LATENT, NOPE), BF16)],
    )(place, mine, other, *blocks)


def stack_kernel(a, b, c, d, out):
    rows = a.shape[0]
    for at, block in enumerate((a, b, c, d)):
        out[at * rows : (at + 1) * rows, :] = block[...]


def stack(blocks):
    rows, width = blocks[0].shape
    return pl.pallas_call(
        stack_kernel,
        out_shape=jax.ShapeDtypeStruct((4 * rows, width), BF16),
        in_specs=[VMEM] * 4,
        out_specs=VMEM,
    )(*blocks)


def fold(op, value):
    so_far = value[:, :128]
    for at in range(128, value.shape[1], 128):
        so_far = op(so_far, value[:, at : at + 128])
    return so_far


def attend_kernel(live_ref, qa, qb, qc, qd, cache, oa, ob, oc, od, query, held, scores, tops, totals, acc, sems, *, block):
    blocks = cache.shape[1] // block
    rows = query.shape[0]
    live = live_ref[0]

    def arrival(i):
        at = pl.ds(pl.multiple_of(i * block, block), block)
        return pltpu.make_async_copy(cache.at[:, at], held.at[:, at], sems.at[i])

    for i in range(blocks):
        arrival(i).start()
    group = qa.shape[0]
    for at, part in enumerate((qa, qb, qc, qd)):
        query[at * group : (at + 1) * group, :] = part[...]
    tops[...] = jnp.full(tops.shape, MASKED, F32)
    totals[...] = jnp.zeros(totals.shape, F32)
    acc[...] = jnp.zeros(acc.shape, F32)

    def score(i, masked):
        start = pl.multiple_of(i * block, block)
        at = pl.ds(start, block)
        arrival(i).wait()
        s = jnp.dot(query[...], held[:, at], preferred_element_type=F32)
        if masked:
            s = jnp.where(start + lax.broadcasted_iota(jnp.int32, s.shape, 1) < live, s, MASKED)
        scores[:, at] = s
        tops[...] = jnp.maximum(tops[...], fold(jnp.maximum, s))

    def top_of():
        high, low = two_terms(jnp.max(tops[...], axis=1, keepdims=True) * TO_LOG2)
        return high + low

    def weigh(i, top):
        at = pl.ds(pl.multiple_of(i * block, block), block)
        p = jnp.exp2(scores[:, at] * TO_LOG2 - top)
        totals[...] += fold(jnp.add, p)
        acc[...] += lax.dot_general(
            p.astype(BF16), held[:LATENT, at], (((1,), (1,)), ((), ())), preferred_element_type=F32
        )

    def loop(first, last, body):
        lax.fori_loop(first, last, lambda i, c: (body(i), c)[1], 0)

    full = live >= blocks * block

    @pl.when(full)
    def _():
        loop(0, blocks, lambda i: score(i, False))
        top = top_of()
        loop(0, blocks, lambda i: weigh(i, top))

    @pl.when(jnp.logical_not(full))
    def _():
        some = (live + block - 1) // block
        loop(0, some, lambda i: score(i, True))
        loop(some, blocks, lambda i: arrival(i).wait())
        top = top_of()
        loop(0, some, lambda i: weigh(i, top))

    total = jnp.sum(totals[...], axis=1, keepdims=True)
    normal = (acc[...] * jnp.where(total > 0, 1.0 / total, 0.0)).astype(BF16)
    stats = pack_stats(top_of(), total, rows)
    for at, out in enumerate((oa, ob, oc, od)):
        out[:, :LATENT] = normal[at * group : (at + 1) * group]
        out[:, LATENT:] = stats[at * group : (at + 1) * group]


def attend(live, parts, cache, block=2048):
    group = parts[0].shape[0]
    rows, span = group * len(parts), cache.shape[1]
    return pl.pallas_call(
        functools.partial(attend_kernel, block=block),
        out_shape=[jax.ShapeDtypeStruct((group, PAYLOAD), BF16)] * 4,
        in_specs=[SMEM] + [VMEM] * 4 + [ANY],
        out_specs=[VMEM] * 4,
        scratch_shapes=[
            pltpu.VMEM((rows, WIDTH), BF16),
            pltpu.VMEM((WIDTH, span), BF16),
            pltpu.VMEM((rows, span), F32),
            pltpu.VMEM((rows, 128), F32),
            pltpu.VMEM((rows, 128), F32),
            pltpu.VMEM((rows, LATENT), F32),
            pltpu.SemaphoreType.DMA((span // block,)),
        ],
        compiler_params=pltpu.CompilerParams(vmem_limit_bytes=56 * 2**20),
        cost_estimate=pl.CostEstimate(
            flops=2 * rows * span * (WIDTH + LATENT), bytes_accessed=span * WIDTH * 2, transcendentals=rows * span
        ),
    )(live, *parts, cache)


def merge_kernel(a, b, c, d, oa, ob, oc, od):
    out, top, total = merge([a[...], b[...], c[...], d[...]])
    stats = pack_stats(top, total, out.shape[0])
    rows = oa.shape[0]
    for at, part in enumerate((oa, ob, oc, od)):
        here = slice(at * rows, (at + 1) * rows)
        part[:, :LATENT] = out[here].astype(BF16)
        part[:, LATENT:] = stats[here]


def merge_groups(parts):
    rows, width = parts[0].shape
    return pl.pallas_call(
        merge_kernel,
        out_shape=[jax.ShapeDtypeStruct((rows // 4, width), BF16)] * 4,
        in_specs=[VMEM] * 4,
        out_specs=[VMEM] * 4,
    )(*parts)


def finish_kernel(a, b, c, d, weight, out, context):
    context[...] = merge([a[...], b[...], c[...], d[...]])[0].astype(BF16)
    frames, heads, _ = out.shape
    for h in range(heads):
        out[:, h, :] = jnp.dot(
            context[h * frames : (h + 1) * frames, :], weight[h], preferred_element_type=F32
        ).astype(BF16)


def finish(parts, weight, frames):
    heads, _, vhead = weight.shape
    return pl.pallas_call(
        finish_kernel,
        out_shape=jax.ShapeDtypeStruct((frames, heads, vhead), BF16),
        in_specs=[VMEM] * 5,
        out_specs=VMEM,
        scratch_shapes=[pltpu.VMEM(parts[0].shape[:1] + (LATENT,), BF16)],
    )(*parts, weight)


def on_device(queries, latent_cache, lengths, key_weight, value_weight):
    frames, heads, _ = queries.shape[1:]
    roll, seq = lax.axis_index("roll"), lax.axis_index("seq")
    place = jnp.stack([roll // CORES, roll % CORES]).astype(jnp.int32)
    span = latent_cache.shape[1]
    live = jnp.clip(lengths - seq * span, 0, span).astype(jnp.int32)
    cache = latent_cache[0].T
    value_all = lax.all_gather(value_weight, "roll", axis=1, tiled=True)

    mine = queries[0]
    block = jnp.swapaxes(key_weight, 1, 2)
    blocks = [block] + [y_shift(block, hops) for hops in (1, 2, 3)]
    other = core_swap(mine)
    own, others = absorb(place, mine, other, blocks)
    local = (own + core_swap(others)).reshape(heads * frames, WIDTH)

    near = stack([local] + [z_shift(local, hops) for hops in (1, 2, 3)])
    groups = [near] + [x_shift(near, hops) for hops in (1, 2, 3)]

    parts = attend(live, groups, cache)

    near = merge_groups([parts[0]] + [x_shift(parts[hops], -hops) for hops in (1, 2, 3)])
    last = [near[0]] + [z_shift(near[hops], -hops) for hops in (1, 2, 3)]
    return finish(last, value_all, frames)[None]


def solution(mesh):
    placed = (
        P("roll", None, "seq", None),
        P("roll", "seq", None),
        P("roll"),
        P("seq", None, "roll"),
        P("seq", "roll", None),
    )
    return jax.shard_map(
        on_device,
        mesh=mesh,
        in_specs=placed,
        out_specs=P("roll", None, "seq", None),
        check_vma=False,
    )
```

```python
import functools

import jax
import jax.numpy as jnp
from jax import lax
from jax.experimental import pallas as pl
from jax.experimental.pallas import tpu as pltpu
from jax.sharding import PartitionSpec as P

NOPE = 128
ROPE = 64
LATENT = 512
WIDTH = LATENT + ROPE
PAYLOAD = LATENT + 128
RING = 4
CORES = 2

MASKED = -1e30
TO_LOG2 = (NOPE + ROPE) ** (-0.5) * 1.4426950408889634

VMEM = pl.BlockSpec(memory_space=pltpu.VMEM)
HBM = pl.BlockSpec(memory_space=pltpu.HBM)
SMEM = pl.BlockSpec(memory_space=pltpu.SMEM)
BF16 = jnp.bfloat16
F32 = jnp.float32


def exchange(value, move):
    pairs = []
    for y in range(RING):
        for core in range(CORES):
            for z in range(RING):
                for x in range(RING):
                    to_y, to_core, to_z, to_x = (at % size for at, size in zip(move(y, core, z, x), (RING, CORES, RING, RING)))
                    source = ((y * CORES + core) * RING + z) * RING + x
                    target = ((to_y * CORES + to_core) * RING + to_z) * RING + to_x
                    pairs.append((source, target))
    return lax.ppermute(value, ("roll", "seq"), pairs)


def core_swap(value):
    return exchange(value, lambda y, core, z, x: (y, core + 1, z, x))


def y_shift(value, hops):
    return exchange(value, lambda y, core, z, x: (y + hops, core, z, x))


def first_shift(value, hops):
    return exchange(value, lambda y, core, z, x: (y, core, z + hops * (1 - core), x + hops * core))


def second_shift(value, hops):
    return exchange(value, lambda y, core, z, x: (y, core, z + hops * core, x + hops * (1 - core)))


def two_terms(value):
    high = value.astype(BF16).astype(F32)
    return high, (value - high).astype(BF16).astype(F32)


def pack_stats(top, total):
    lane = lax.broadcasted_iota(jnp.int32, top.shape, 1)
    packed = jnp.zeros(top.shape, F32)
    for at, term in enumerate(two_terms(top) + two_terms(total)):
        packed = jnp.where(lane == at, term, packed)
    return packed.astype(BF16)


def spread(stats, first):
    row = lax.broadcasted_iota(jnp.int32, (128, 128), 0)
    chosen = ((row == first) | (row == first + 1)).astype(F32).astype(BF16)
    return jnp.dot(stats, chosen, preferred_element_type=F32)


def merge(parts):
    tops = [spread(part[:, LATENT:], 0) for part in parts]
    totals = [spread(part[:, LATENT:], 2) for part in parts]
    top = functools.reduce(jnp.maximum, tops)
    weights = [jnp.exp2(t - top) * n for t, n in zip(tops, totals)]
    total = functools.reduce(jnp.add, weights)
    inverse = jnp.where(total > 0, 1.0 / total, 0.0)
    weights = [w * inverse for w in weights]
    columns = []
    for at in range(0, LATENT, 128):
        terms = [part[:, at : at + 128].astype(F32) * w for part, w in zip(parts, weights)]
        columns.append(functools.reduce(jnp.add, terms))
    return columns, top, total


def load_kernel(cache, block, query, value, *refs):
    sources, targets, sems = (cache, block, query, value), refs[:4], refs[4]
    copies = [pltpu.make_async_copy(a, b, sems.at[i]) for i, (a, b) in enumerate(zip(sources, targets))]
    for copy in copies:
        copy.start()
    for copy in copies:
        copy.wait()


def load(*arrays):
    return pl.pallas_call(
        load_kernel,
        out_shape=[jax.ShapeDtypeStruct(a.shape, a.dtype) for a in arrays],
        in_specs=[HBM] * 4,
        out_specs=[VMEM] * 4,
        scratch_shapes=[pltpu.SemaphoreType.DMA((4,))],
        compiler_params=pltpu.CompilerParams(vmem_limit_bytes=16 * 2**20),
        cost_estimate=pl.CostEstimate(
            flops=0, bytes_accessed=2 * sum(a.size * 2 for a in arrays), transcendentals=0
        ),
    )(*arrays)


def absorb_kernel(mine, other, kw0, kw1, kw2, kw3, out_mine, out_other, weights):
    roll = lax.axis_index("roll")
    y, core = roll // CORES, lax.rem(roll, CORES)
    frames, heads, _ = mine.shape
    weights[...] = jnp.zeros_like(weights)
    for hops, block in enumerate((kw0, kw1, kw2, kw3)):
        chunk = lax.rem(y + RING - hops, RING) * CORES + core
        weights[:, pl.ds(pl.multiple_of(chunk * 64, 64), 64), :] = block[...]
    absorbed = []
    for h in range(heads):
        rows = jnp.concatenate([mine[:, h, :NOPE], other[:, h, :NOPE]], axis=0)
        absorbed.append(
            lax.dot_general(rows, weights[h], (((1,), (1,)), ((), ())), preferred_element_type=F32)
        )
    out_mine[:, :LATENT] = jnp.concatenate([a[:frames] for a in absorbed], axis=0).astype(BF16)
    out_other[:, :LATENT] = jnp.concatenate([a[frames:] for a in absorbed], axis=0).astype(BF16)
    out_other[:, LATENT:] = jnp.zeros((heads * frames, ROPE), BF16)
    rope = [mine[:, h, NOPE:].astype(F32) for h in range(heads)]
    out_mine[:, LATENT:] = jnp.concatenate(rope, axis=0).astype(BF16)


def absorb(mine, other, blocks):
    frames, heads, _ = mine.shape
    shape = jax.ShapeDtypeStruct((heads * frames, WIDTH), BF16)
    return pl.pallas_call(
        absorb_kernel,
        out_shape=[shape, shape],
        in_specs=[VMEM] * 6,
        out_specs=[VMEM, VMEM],
        scratch_shapes=[pltpu.VMEM((heads, LATENT, NOPE), BF16)],
    )(mine, other, *blocks)


def stack_kernel(a, b, c, d, out):
    rows = a.shape[0]
    for at, block in enumerate((a, b, c, d)):
        out[at * rows : (at + 1) * rows, :] = block[...]


def stack(blocks):
    rows, width = blocks[0].shape
    return pl.pallas_call(
        stack_kernel,
        out_shape=jax.ShapeDtypeStruct((4 * rows, width), BF16),
        in_specs=[VMEM] * 4,
        out_specs=VMEM,
    )(*blocks)


def fold(op, value):
    so_far = value[:, :128]
    for at in range(128, value.shape[1], 128):
        so_far = op(so_far, value[:, at : at + 128])
    return so_far


def attend_kernel(length, qa, qb, cache, oa, ob, query, scores, tops, totals, acc, *, block):
    span = cache.shape[1]
    blocks = span // block
    live = jnp.clip(length[0] - lax.axis_index("seq") * span, 0, span)
    group = qa.shape[0]
    query[:group, :] = qa[...]
    query[group:, :] = qb[...]

    def here(i):
        return pl.ds(i * block if isinstance(i, int) else pl.multiple_of(i * block, block), block)

    def score(i):
        return jnp.dot(query[...], cache[:, here(i)], preferred_element_type=F32)

    def weigh(i, p):
        return lax.dot_general(
            p.astype(BF16), cache[:LATENT, here(i)], (((1,), (1,)), ((), ())), preferred_element_type=F32
        )

    def largest(value):
        return jnp.broadcast_to(jnp.max(value, axis=1, keepdims=True), value.shape)

    def finish(top):
        total = jnp.broadcast_to(jnp.sum(totals[...], axis=1, keepdims=True), totals.shape)
        inverse = jnp.where(total > 0, 1.0 / total, 0.0)
        high, low = two_terms(top)
        sent = high + low
        stats = pack_stats(sent, total * jnp.exp2(top - sent))
        for at, out in enumerate((oa, ob)):
            rows = slice(at * group, (at + 1) * group)
            for column in range(0, LATENT, 128):
                lanes = slice(column, column + 128)
                out[:, lanes] = (acc[rows, lanes] * inverse[rows]).astype(BF16)
            out[:, LATENT:] = stats[rows]

    def scaled(value, factor):
        return jnp.concatenate([value[:, at : at + 128] * factor for at in range(0, LATENT, 128)], axis=1)

    @pl.when(live >= span)
    def _():
        scores[:, here(0)] = score(0)
        for i in range(blocks):
            s = scores[:, here(i % 2)]
            if i + 1 < blocks:
                scores[:, here((i + 1) % 2)] = score(i + 1)
            block_top = largest(fold(jnp.maximum, s)) * TO_LOG2
            top = block_top if i == 0 else jnp.maximum(tops[...], block_top)
            p = jnp.exp2(s * TO_LOG2 - top[:, :1])
            if i == 0:
                totals[...] = fold(jnp.add, p)
                acc[...] = weigh(i, p)
            else:
                factor = jnp.exp2(tops[...] - top)
                totals[...] = totals[...] * factor + fold(jnp.add, p)
                acc[...] = scaled(acc[...], factor) + weigh(i, p)
            tops[...] = top
        finish(tops[...])

    @pl.when(live < span)
    def _():
        whole = live // block
        some = (live + block - 1) // block
        tops[...] = jnp.full(tops.shape, MASKED, F32)
        totals[...] = jnp.zeros(totals.shape, F32)
        acc[...] = jnp.zeros(acc.shape, F32)

        def fill(i, masked):
            s = score(i)
            if masked:
                s = jnp.where(i * block + lax.broadcasted_iota(jnp.int32, s.shape, 1) < live, s, MASKED)
            scores[:, here(i)] = s
            tops[...] = jnp.maximum(tops[...], fold(jnp.maximum, s))

        def loop(first, last, body):
            lax.fori_loop(first, last, lambda i, c: (body(i), c)[1], 0)

        loop(0, whole, lambda i: fill(i, False))
        loop(whole, some, lambda i: fill(i, True))
        top = largest(tops[...]) * TO_LOG2

        def add(i):
            p = jnp.exp2(scores[:, here(i)] * TO_LOG2 - top[:, :1])
            totals[...] += fold(jnp.add, p)
            acc[...] += weigh(i, p)

        loop(0, some, add)
        finish(top)


def attend(length, parts, cache, block=1024):
    group = parts[0].shape[0]
    rows, span = group * len(parts), cache.shape[1]
    return pl.pallas_call(
        functools.partial(attend_kernel, block=block),
        out_shape=[jax.ShapeDtypeStruct((group, PAYLOAD), BF16)] * 2,
        in_specs=[SMEM] + [VMEM] * 3,
        out_specs=[VMEM] * 2,
        scratch_shapes=[
            pltpu.VMEM((rows, WIDTH), BF16),
            pltpu.VMEM((rows, span), F32),
            pltpu.VMEM((rows, 128), F32),
            pltpu.VMEM((rows, 128), F32),
            pltpu.VMEM((rows, LATENT), F32),
        ],
        compiler_params=pltpu.CompilerParams(vmem_limit_bytes=24 * 2**20),
        cost_estimate=pl.CostEstimate(
            flops=2 * rows * span * (WIDTH + LATENT), bytes_accessed=span * WIDTH * 2, transcendentals=rows * span
        ),
    )(length, *parts, cache)


def merge_kernel(a, b, c, d, oa, ob, oc, od):
    columns, top, total = merge([a, b, c, d])
    stats = pack_stats(top, total)
    rows = oa.shape[0]
    for at, part in enumerate((oa, ob, oc, od)):
        here = slice(at * rows, (at + 1) * rows)
        for j, column in enumerate(columns):
            part[:, j * 128 : (j + 1) * 128] = column[here].astype(BF16)
        part[:, LATENT:] = stats[here]


def merge_groups(parts):
    rows, width = parts[0].shape
    return pl.pallas_call(
        merge_kernel,
        out_shape=[jax.ShapeDtypeStruct((rows // 4, width), BF16)] * 4,
        in_specs=[VMEM] * 4,
        out_specs=[VMEM] * 4,
    )(*parts)


def pair_kernel(mine, other, out):
    core = lax.rem(lax.axis_index("roll"), CORES)
    out[core] = mine[...]
    out[1 - core] = other[...]


def pair(mine, other):
    return pl.pallas_call(
        pair_kernel,
        out_shape=jax.ShapeDtypeStruct((CORES,) + mine.shape, BF16),
        in_specs=[VMEM, VMEM],
        out_specs=VMEM,
    )(mine, other)


def finish_kernel(a, b, c, d, w0, w1, w2, w3, out, context, weight):
    y = lax.axis_index("roll") // CORES
    for hops, block in enumerate((w0, w1, w2, w3)):
        chunk = lax.rem(y + RING - hops, RING) * CORES
        for core in range(CORES):
            weight[:, pl.ds(pl.multiple_of((chunk + core) * 64, 64), 64), :] = block[core]
    for j, column in enumerate(merge([a, b, c, d])[0]):
        context[:, j * 128 : (j + 1) * 128] = column.astype(BF16)
    frames, heads, _ = out.shape
    for h in range(heads):
        out[:, h, :] = jnp.dot(
            context[h * frames : (h + 1) * frames, :], weight[h], preferred_element_type=F32
        ).astype(BF16)


def finish(parts, weights, frames):
    _, heads, _, vhead = weights[0].shape
    return pl.pallas_call(
        finish_kernel,
        out_shape=jax.ShapeDtypeStruct((frames, heads, vhead), BF16),
        in_specs=[VMEM] * 8,
        out_specs=VMEM,
        scratch_shapes=[
            pltpu.VMEM((frames * heads, LATENT), BF16),
            pltpu.VMEM((heads, LATENT, vhead), BF16),
        ],
    )(*parts, *weights)


def on_device(queries, latent_cache, lengths, key_weight, value_weight):
    frames = queries.shape[1]
    lengths = lengths.astype(jnp.int32)
    cache, block = latent_cache[0].T, jnp.swapaxes(key_weight, 1, 2)
    mine = queries[0]

    blocks = [y_shift(block, hops) for hops in (1, 2, 3)]
    other, value_other = core_swap(mine), core_swap(value_weight)
    cache, block, mine, value_mine = load(cache, block, mine, value_weight)
    own, others = absorb(mine, other, [block] + blocks)
    value_pair = pair(value_mine, value_other)
    local = own + core_swap(others)

    local, value_pair = lax.optimization_barrier((local, value_pair))
    near = stack([local] + [first_shift(local, hops) for hops in (1, 2, 3)])
    groups = [near] + [second_shift(near, hops) for hops in (1, 2, 3)]
    value_pairs = [value_pair] + [y_shift(value_pair, hops) for hops in (1, 2, 3)]

    early = attend(lengths, groups[:2], cache)
    groups, value_pairs = lax.optimization_barrier((groups, value_pairs))
    late = attend(lengths, groups[2:], cache)
    parts = list(early) + list(late)

    near = merge_groups([parts[0]] + [second_shift(parts[hops], -hops) for hops in (1, 2, 3)])
    last = [near[0]] + [first_shift(near[hops], -hops) for hops in (1, 2, 3)]
    return finish(last, value_pairs, frames)[None]


def solution(mesh):
    placed = (
        P("roll", None, "seq", None),
        P("roll", "seq", None),
        P("roll"),
        P("seq", None, "roll"),
        P("seq", "roll", None),
    )
    return jax.shard_map(
        on_device,
        mesh=mesh,
        in_specs=placed,
        out_specs=P("roll", None, "seq", None),
        check_vma=False,
    )
```

```python
import functools

import jax
import jax.numpy as jnp
from jax import lax
from jax.experimental import pallas as pl
from jax.experimental.pallas import tpu as pltpu
from jax.sharding import PartitionSpec as P

NOPE = 128
ROPE = 64
LATENT = 512
WIDTH = LATENT + ROPE
PAYLOAD = LATENT + 128
RING = 4
CORES = 2

MASKED = -1e30
TO_LOG2 = (NOPE + ROPE) ** (-0.5) * 1.4426950408889634

VMEM = pl.BlockSpec(memory_space=pltpu.VMEM)
SMEM = pl.BlockSpec(memory_space=pltpu.SMEM)
SMALL = pltpu.CompilerParams(vmem_limit_bytes=4 * 2**20)
BF16 = jnp.bfloat16
F32 = jnp.float32


def exchange(value, move):
    pairs = []
    for y in range(RING):
        for core in range(CORES):
            for z in range(RING):
                for x in range(RING):
                    to_y, to_core, to_z, to_x = (at % size for at, size in zip(move(y, core, z, x), (RING, CORES, RING, RING)))
                    source = ((y * CORES + core) * RING + z) * RING + x
                    target = ((to_y * CORES + to_core) * RING + to_z) * RING + to_x
                    pairs.append((source, target))
    return lax.ppermute(value, ("roll", "seq"), pairs)


def core_swap(value):
    return exchange(value, lambda y, core, z, x: (y, core + 1, z, x))


def y_shift(value, hops):
    return exchange(value, lambda y, core, z, x: (y + hops, core, z, x))


def y_owners():
    y = lax.axis_index("roll") // CORES
    return [lax.rem(y + RING - hops, RING) for hops in range(RING)]


def first_shift(value, hops):
    return exchange(value, lambda y, core, z, x: (y, core, z + hops * (1 - core), x + hops * core))


def second_shift(value, hops):
    return exchange(value, lambda y, core, z, x: (y, core, z + hops * core, x + hops * (1 - core)))


def two_terms(value):
    high = value.astype(BF16).astype(F32)
    return high, (value - high).astype(BF16).astype(F32)


def pack_stats(top, total):
    lane = lax.broadcasted_iota(jnp.int32, top.shape, 1)
    packed = jnp.zeros(top.shape, F32)
    for at, term in enumerate(two_terms(top) + two_terms(total)):
        packed = jnp.where(lane == at, term, packed)
    return packed.astype(BF16)


def spread(stats, first):
    row = lax.broadcasted_iota(jnp.int32, (128, 128), 0)
    chosen = ((row == first) | (row == first + 1)).astype(F32).astype(BF16)
    return jnp.dot(stats, chosen, preferred_element_type=F32)


def merge(parts):
    tops = [spread(part[:, LATENT:], 0) for part in parts]
    totals = [spread(part[:, LATENT:], 2) for part in parts]
    top = functools.reduce(jnp.maximum, tops)
    weights = [jnp.exp2(t - top) * n for t, n in zip(tops, totals)]
    total = functools.reduce(jnp.add, weights)
    inverse = jnp.where(total > 0, 1.0 / total, 0.0)
    weights = [w * inverse for w in weights]
    columns = []
    for at in range(0, LATENT, 128):
        terms = [part[:, at : at + 128].astype(F32) * w for part, w in zip(parts, weights)]
        columns.append(functools.reduce(jnp.add, terms))
    return columns, top, total


def load_kernel(*refs):
    count = len(refs) // 2
    sems = refs[-1]
    copies = [pltpu.make_async_copy(refs[i], refs[count + i], sems.at[i]) for i in range(count)]
    for copy in copies:
        copy.start()
    for copy in copies:
        copy.wait()


def load(*arrays):
    return pl.pallas_call(
        load_kernel,
        out_shape=[jax.ShapeDtypeStruct(a.shape, a.dtype) for a in arrays],
        in_specs=[pl.BlockSpec(memory_space=pltpu.HBM)] * len(arrays),
        out_specs=[VMEM] * len(arrays),
        scratch_shapes=[pltpu.SemaphoreType.DMA((len(arrays),))],
        compiler_params=SMALL,
        cost_estimate=pl.CostEstimate(
            flops=0, bytes_accessed=2 * sum(a.size * 2 for a in arrays), transcendentals=0
        ),
    )(*[pltpu.with_memory_space_constraint(a, pltpu.HBM) for a in arrays])


def absorb_kernel(mine, other, kw0, kw1, kw2, kw3, out_mine, out_other, weights):
    core = lax.rem(lax.axis_index("roll"), CORES)
    frames, heads, _ = mine.shape
    weights[...] = jnp.zeros_like(weights)
    for owner, block in zip(y_owners(), (kw0, kw1, kw2, kw3)):
        chunk = owner * CORES + core
        weights[:, pl.ds(pl.multiple_of(chunk * 64, 64), 64), :] = block[...]
    absorbed = []
    for h in range(heads):
        rows = jnp.concatenate([mine[:, h, :NOPE], other[:, h, :NOPE]], axis=0)
        absorbed.append(
            lax.dot_general(rows, weights[h], (((1,), (1,)), ((), ())), preferred_element_type=F32)
        )
    out_mine[:, :LATENT] = jnp.concatenate([a[:frames] for a in absorbed], axis=0).astype(BF16)
    out_other[:, :LATENT] = jnp.concatenate([a[frames:] for a in absorbed], axis=0).astype(BF16)
    out_other[:, LATENT:] = jnp.zeros((heads * frames, ROPE), BF16)
    rope = [mine[:, h, NOPE:].astype(F32) for h in range(heads)]
    out_mine[:, LATENT:] = jnp.concatenate(rope, axis=0).astype(BF16)


def absorb(mine, other, blocks):
    frames, heads, _ = mine.shape
    shape = jax.ShapeDtypeStruct((heads * frames, WIDTH), BF16)
    return pl.pallas_call(
        absorb_kernel,
        out_shape=[shape, shape],
        in_specs=[VMEM] * 6,
        out_specs=[VMEM, VMEM],
        scratch_shapes=[pltpu.VMEM((heads, LATENT, NOPE), BF16)],
        compiler_params=SMALL,
    )(mine, other, *blocks)


def stack_kernel(*refs):
    parts, out = refs[:-1], refs[-1]
    rows = parts[0].shape[0]
    for at, part in enumerate(parts):
        out[at * rows : (at + 1) * rows, :] = part[...]


def stack(parts):
    rows, width = parts[0].shape
    return pl.pallas_call(
        stack_kernel,
        out_shape=jax.ShapeDtypeStruct((len(parts) * rows, width), BF16),
        in_specs=[VMEM] * len(parts),
        out_specs=VMEM,
        compiler_params=SMALL,
    )(*parts)


def fold(op, value):
    so_far = value[:, :128]
    for at in range(128, value.shape[1], 128):
        so_far = op(so_far, value[:, at : at + 128])
    return so_far


def attend_kernel(length, cache, *refs, block):
    count = (len(refs) - 5) // 2
    parts, outs = refs[:count], refs[count : 2 * count]
    query, scores, tops, totals, acc = refs[2 * count :]
    span = cache.shape[1]
    blocks = span // block
    live = jnp.clip(length[0] - lax.axis_index("seq") * span, 0, span)
    group = parts[0].shape[0]
    for at, part in enumerate(parts):
        query[at * group : (at + 1) * group, :] = part[...]

    def here(i):
        return pl.ds(i * block if isinstance(i, int) else pl.multiple_of(i * block, block), block)

    def score(i):
        return jnp.dot(query[...], cache[:, here(i)], preferred_element_type=F32)

    def weigh(i, p):
        return lax.dot_general(
            p.astype(BF16), cache[:LATENT, here(i)], (((1,), (1,)), ((), ())), preferred_element_type=F32
        )

    def largest(value):
        return jnp.broadcast_to(jnp.max(value, axis=1, keepdims=True), value.shape)

    def finish(top):
        total = jnp.broadcast_to(jnp.sum(totals[...], axis=1, keepdims=True), totals.shape)
        inverse = jnp.where(total > 0, 1.0 / total, 0.0)
        high, low = two_terms(top)
        sent = high + low
        stats = pack_stats(sent, total * jnp.exp2(top - sent))
        for at, out in enumerate(outs):
            rows = slice(at * group, (at + 1) * group)
            for column in range(0, LATENT, 128):
                lanes = slice(column, column + 128)
                out[:, lanes] = (acc[rows, lanes] * inverse[rows]).astype(BF16)
            out[:, LATENT:] = stats[rows]

    def scaled(value, factor):
        return jnp.concatenate([value[:, at : at + 128] * factor for at in range(0, LATENT, 128)], axis=1)

    @pl.when(live >= span)
    def _():
        scores[:, here(0)] = score(0)
        for i in range(blocks):
            s = scores[:, here(i % 2)]
            if i + 1 < blocks:
                scores[:, here((i + 1) % 2)] = score(i + 1)
            block_top = largest(fold(jnp.maximum, s)) * TO_LOG2
            top = block_top if i == 0 else jnp.maximum(tops[...], block_top)
            p = jnp.exp2(s * TO_LOG2 - top[:, :1])
            if i == 0:
                totals[...] = fold(jnp.add, p)
                acc[...] = weigh(i, p)
            else:
                factor = jnp.exp2(tops[...] - top)
                totals[...] = totals[...] * factor + fold(jnp.add, p)
                acc[...] = scaled(acc[...], factor) + weigh(i, p)
            tops[...] = top
        finish(tops[...])

    @pl.when(live < span)
    def _():
        whole = live // block
        some = (live + block - 1) // block
        tops[...] = jnp.full(tops.shape, MASKED, F32)
        totals[...] = jnp.zeros(totals.shape, F32)
        acc[...] = jnp.zeros(acc.shape, F32)

        def fill(i, masked):
            s = score(i)
            if masked:
                s = jnp.where(i * block + lax.broadcasted_iota(jnp.int32, s.shape, 1) < live, s, MASKED)
            scores[:, here(i)] = s
            tops[...] = jnp.maximum(tops[...], fold(jnp.maximum, s))

        def loop(first, last, body):
            lax.fori_loop(first, last, lambda i, c: (body(i), c)[1], 0)

        loop(0, whole, lambda i: fill(i, False))
        loop(whole, some, lambda i: fill(i, True))
        top = largest(tops[...]) * TO_LOG2

        def add(i):
            p = jnp.exp2(scores[:, here(i)] * TO_LOG2 - top[:, :1])
            totals[...] += fold(jnp.add, p)
            acc[...] += weigh(i, p)

        loop(0, some, add)
        finish(top)


def attend(length, parts, cache, block=1024):
    group = parts[0].shape[0]
    rows, span = group * len(parts), cache.shape[1]
    return pl.pallas_call(
        functools.partial(attend_kernel, block=block),
        out_shape=[jax.ShapeDtypeStruct((group, PAYLOAD), BF16)] * len(parts),
        in_specs=[SMEM] + [VMEM] * (1 + len(parts)),
        out_specs=[VMEM] * len(parts),
        scratch_shapes=[
            pltpu.VMEM((rows, WIDTH), BF16),
            pltpu.VMEM((rows, span), F32),
            pltpu.VMEM((rows, 128), F32),
            pltpu.VMEM((rows, 128), F32),
            pltpu.VMEM((rows, LATENT), F32),
        ],
        compiler_params=pltpu.CompilerParams(vmem_limit_bytes=24 * 2**20),
        cost_estimate=pl.CostEstimate(
            flops=2 * rows * span * (WIDTH + LATENT), bytes_accessed=span * WIDTH * 2, transcendentals=rows * span
        ),
    )(length, cache, *parts)


def merge_kernel(*refs):
    parts, outs = refs[:RING], refs[RING:]
    columns, top, total = merge(parts)
    stats = pack_stats(top, total)
    rows = outs[0].shape[0]
    for at, out in enumerate(outs):
        here = slice(at * rows, (at + 1) * rows)
        for j, column in enumerate(columns):
            out[:, j * 128 : (j + 1) * 128] = column[here].astype(BF16)
        out[:, LATENT:] = stats[here]


def merge_groups(parts):
    rows, width = parts[0].shape
    return pl.pallas_call(
        merge_kernel,
        out_shape=[jax.ShapeDtypeStruct((rows // RING, width), BF16)] * RING,
        in_specs=[VMEM] * RING,
        out_specs=[VMEM] * RING,
        compiler_params=SMALL,
    )(*parts)


def pair_kernel(mine, other, out):
    core = lax.rem(lax.axis_index("roll"), CORES)
    out[core] = mine[...]
    out[1 - core] = other[...]


def pair(mine, other):
    return pl.pallas_call(
        pair_kernel,
        out_shape=jax.ShapeDtypeStruct((CORES,) + mine.shape, BF16),
        in_specs=[VMEM, VMEM],
        out_specs=VMEM,
        compiler_params=SMALL,
    )(mine, other)


def finish_kernel(a, b, c, d, w0, w1, w2, w3, out, context, weight):
    for owner, block in zip(y_owners(), (w0, w1, w2, w3)):
        for core in range(CORES):
            weight[:, pl.ds(pl.multiple_of((owner * CORES + core) * 64, 64), 64), :] = block[core]
    for j, column in enumerate(merge([a, b, c, d])[0]):
        context[:, j * 128 : (j + 1) * 128] = column.astype(BF16)
    frames, heads, _ = out.shape
    for h in range(heads):
        out[:, h, :] = jnp.dot(
            context[h * frames : (h + 1) * frames, :], weight[h], preferred_element_type=F32
        ).astype(BF16)


def finish(parts, weights, frames):
    _, heads, _, vhead = weights[0].shape
    return pl.pallas_call(
        finish_kernel,
        out_shape=jax.ShapeDtypeStruct((frames, heads, vhead), BF16),
        in_specs=[VMEM] * 8,
        out_specs=VMEM,
        scratch_shapes=[
            pltpu.VMEM((frames * heads, LATENT), BF16),
            pltpu.VMEM((heads, LATENT, vhead), BF16),
        ],
        compiler_params=SMALL,
    )(*parts, *weights)


def on_device(queries, latent_cache, lengths, key_weight, value_weight):
    frames = queries.shape[1]
    lengths = lengths.astype(jnp.int32)
    cache, block = latent_cache[0].T, jnp.swapaxes(key_weight, 1, 2)
    mine = queries[0]

    blocks = [y_shift(block, hops) for hops in (1, 2, 3)]
    other, value_other = core_swap(mine), core_swap(value_weight)
    cache, block, mine, value_mine = load(cache, block, mine, value_weight)
    own, others = absorb(mine, other, [block] + blocks)
    value_pair = pair(value_mine, value_other)
    local = own + core_swap(others)

    local, value_pair = lax.optimization_barrier((local, value_pair))
    near = stack([local] + [first_shift(local, hops) for hops in (1, 2, 3)])
    groups = [near] + [second_shift(near, hops) for hops in (1, 2, 3)]
    value_pairs = [value_pair] + [y_shift(value_pair, hops) for hops in (1, 2, 3)]

    one, three = attend(lengths, [groups[1], groups[3]], cache)
    groups, value_pairs = lax.optimization_barrier((groups, value_pairs))
    (two,) = attend(lengths, [groups[2]], cache)
    (zero,) = attend(lengths, [groups[0]], cache)
    parts = [zero] + [second_shift(part, -hops) for hops, part in ((1, one), (2, two), (3, three))]

    near = merge_groups(parts)
    last = [near[0]] + [first_shift(near[hops], -hops) for hops in (1, 2, 3)]
    return finish(last, value_pairs, frames)[None]


def solution(mesh):
    placed = (
        P("roll", None, "seq", None),
        P("roll", "seq", None),
        P("roll"),
        P("seq", None, "roll"),
        P("seq", "roll", None),
    )
    return jax.shard_map(
        on_device,
        mesh=mesh,
        in_specs=placed,
        out_specs=P("roll", None, "seq", None),
        check_vma=False,
    )
```

```python
import functools

import jax
import jax.numpy as jnp
from jax import lax
from jax.experimental import pallas as pl
from jax.experimental.pallas import tpu as pltpu
from jax.sharding import PartitionSpec as P

NOPE = 128
ROPE = 64
LATENT = 512
WIDTH = LATENT + ROPE
PAYLOAD = LATENT + 128
RING = 4
CORES = 2

MASKED = -(2.0**100)
TO_LOG2 = (NOPE + ROPE) ** (-0.5) * 1.4426950408889634

VMEM = pl.BlockSpec(memory_space=pltpu.VMEM)
SMEM = pl.BlockSpec(memory_space=pltpu.SMEM)
SMALL = pltpu.CompilerParams(vmem_limit_bytes=4 * 2**20)
BF16 = jnp.bfloat16
F32 = jnp.float32


def exchange(value, move):
    pairs = []
    for y in range(RING):
        for core in range(CORES):
            for z in range(RING):
                for x in range(RING):
                    to_y, to_core, to_z, to_x = (at % size for at, size in zip(move(y, core, z, x), (RING, CORES, RING, RING)))
                    source = ((y * CORES + core) * RING + z) * RING + x
                    target = ((to_y * CORES + to_core) * RING + to_z) * RING + to_x
                    pairs.append((source, target))
    return lax.ppermute(value, ("roll", "seq"), pairs)


def core_swap(value):
    return exchange(value, lambda y, core, z, x: (y, core + 1, z, x))


def y_shift(value, hops):
    return exchange(value, lambda y, core, z, x: (y + hops, core, z, x))


def y_owners():
    y = lax.axis_index("roll") // CORES
    return [lax.rem(y + RING - hops, RING) for hops in range(RING)]


def first_shift(value, hops):
    return exchange(value, lambda y, core, z, x: (y, core, z + hops * (1 - core), x + hops * core))


def second_shift(value, hops):
    return exchange(value, lambda y, core, z, x: (y, core, z + hops * core, x + hops * (1 - core)))


def two_terms(value):
    high = value.astype(BF16).astype(F32)
    return high, (value - high).astype(BF16).astype(F32)


def pack_stats(top, total):
    lane = lax.broadcasted_iota(jnp.int32, top.shape, 1)
    packed = jnp.zeros(top.shape, F32)
    for at, term in enumerate(two_terms(top) + two_terms(total)):
        packed = jnp.where(lane == at, term, packed)
    return packed.astype(BF16)


def spread(stats, first):
    row = lax.broadcasted_iota(jnp.int32, (128, 128), 0)
    chosen = ((row == first) | (row == first + 1)).astype(F32).astype(BF16)
    return jnp.dot(stats, chosen, preferred_element_type=F32)


def merge(parts):
    tops = [spread(part[:, LATENT:], 0) for part in parts]
    totals = [spread(part[:, LATENT:], 2) for part in parts]
    top = functools.reduce(jnp.maximum, tops)
    weights = [jnp.exp2(t - top) * n for t, n in zip(tops, totals)]
    total = functools.reduce(jnp.add, weights)
    inverse = jnp.where(total > 0, 1.0 / total, 0.0)
    weights = [w * inverse for w in weights]
    columns = []
    for at in range(0, LATENT, 128):
        terms = [part[:, at : at + 128].astype(F32) * w for part, w in zip(parts, weights)]
        columns.append(functools.reduce(jnp.add, terms))
    return columns, top, total


def load_kernel(*refs):
    count = len(refs) // 2
    sems = refs[-1]
    copies = [pltpu.make_async_copy(refs[i], refs[count + i], sems.at[i]) for i in range(count)]
    for copy in copies:
        copy.start()
    for copy in copies:
        copy.wait()


def load(*arrays):
    return pl.pallas_call(
        load_kernel,
        out_shape=[jax.ShapeDtypeStruct(a.shape, a.dtype) for a in arrays],
        in_specs=[pl.BlockSpec(memory_space=pltpu.HBM)] * len(arrays),
        out_specs=[VMEM] * len(arrays),
        scratch_shapes=[pltpu.SemaphoreType.DMA((len(arrays),))],
        compiler_params=SMALL,
        cost_estimate=pl.CostEstimate(
            flops=0, bytes_accessed=2 * sum(a.size * 2 for a in arrays), transcendentals=0
        ),
    )(*[pltpu.with_memory_space_constraint(a, pltpu.HBM) for a in arrays])


def absorb_kernel(mine, other, kw0, kw1, kw2, kw3, out_mine, out_other, weights):
    core = lax.rem(lax.axis_index("roll"), CORES)
    frames, heads, _ = mine.shape
    weights[...] = jnp.zeros_like(weights)
    for owner, block in zip(y_owners(), (kw0, kw1, kw2, kw3)):
        chunk = owner * CORES + core
        weights[:, pl.ds(pl.multiple_of(chunk * 64, 64), 64), :] = block[...]
    absorbed = []
    for h in range(heads):
        rows = jnp.concatenate([mine[:, h, :NOPE], other[:, h, :NOPE]], axis=0)
        absorbed.append(
            lax.dot_general(rows, weights[h], (((1,), (1,)), ((), ())), preferred_element_type=F32)
        )
    out_mine[:, :LATENT] = jnp.concatenate([a[:frames] for a in absorbed], axis=0).astype(BF16)
    out_other[:, :LATENT] = jnp.concatenate([a[frames:] for a in absorbed], axis=0).astype(BF16)
    out_other[:, LATENT:] = jnp.zeros((heads * frames, ROPE), BF16)
    rope = [mine[:, h, NOPE:].astype(F32) for h in range(heads)]
    out_mine[:, LATENT:] = jnp.concatenate(rope, axis=0).astype(BF16)


def absorb(mine, other, blocks):
    frames, heads, _ = mine.shape
    shape = jax.ShapeDtypeStruct((heads * frames, WIDTH), BF16)
    return pl.pallas_call(
        absorb_kernel,
        out_shape=[shape, shape],
        in_specs=[VMEM] * 6,
        out_specs=[VMEM, VMEM],
        scratch_shapes=[pltpu.VMEM((heads, LATENT, NOPE), BF16)],
        compiler_params=SMALL,
    )(mine, other, *blocks)


def stack_kernel(*refs):
    parts, out = refs[:-1], refs[-1]
    rows = parts[0].shape[0]
    for at, part in enumerate(parts):
        out[at * rows : (at + 1) * rows, :] = part[...]


def stack(parts):
    rows, width = parts[0].shape
    return pl.pallas_call(
        stack_kernel,
        out_shape=jax.ShapeDtypeStruct((len(parts) * rows, width), BF16),
        in_specs=[VMEM] * len(parts),
        out_specs=VMEM,
        compiler_params=SMALL,
    )(*parts)


def fold(op, value):
    so_far = value[:, :128]
    for at in range(128, value.shape[1], 128):
        so_far = op(so_far, value[:, at : at + 128])
    return so_far


def attend_kernel(length, cache, *refs, block):
    count = (len(refs) - 5) // 2
    parts, outs = refs[:count], refs[count : 2 * count]
    query, scores, tops, totals, acc = refs[2 * count :]
    span = cache.shape[1]
    blocks = span // block
    live = jnp.clip(length[0] - lax.axis_index("seq") * span, 0, span)
    group = parts[0].shape[0]
    for at, part in enumerate(parts):
        query[at * group : (at + 1) * group, :] = part[...]

    def here(i):
        return pl.ds(i * block if isinstance(i, int) else pl.multiple_of(i * block, block), block)

    def score(i):
        return jnp.dot(query[...], cache[:, here(i)], preferred_element_type=F32)

    def weigh(i, p):
        return lax.dot_general(
            p.astype(BF16), cache[:LATENT, here(i)], (((1,), (1,)), ((), ())), preferred_element_type=F32
        )

    def largest(value):
        return jnp.broadcast_to(jnp.max(value, axis=1, keepdims=True), value.shape)

    def finish(top):
        total = jnp.broadcast_to(jnp.sum(totals[...], axis=1, keepdims=True), totals.shape)
        inverse = jnp.where(total > 0, 1.0 / total, 0.0)
        high, low = two_terms(top)
        sent = high + low
        stats = pack_stats(sent, total * jnp.exp2(top - sent))
        for at, out in enumerate(outs):
            rows = slice(at * group, (at + 1) * group)
            for column in range(0, LATENT, 128):
                lanes = slice(column, column + 128)
                out[:, lanes] = (acc[rows, lanes] * inverse[rows]).astype(BF16)
            out[:, LATENT:] = stats[rows]

    def scaled(value, factor):
        return jnp.concatenate([value[:, at : at + 128] * factor for at in range(0, LATENT, 128)], axis=1)

    def one_pass(masked):
        scores[:, here(0)] = score(0)
        for i in range(blocks):
            s = scores[:, here(i % 2)]
            if i + 1 < blocks:
                scores[:, here((i + 1) % 2)] = score(i + 1)
            if masked:
                column = lax.broadcasted_iota(jnp.int32, s.shape, 1)
                s = jnp.where(column < live - i * block, s, MASKED)
            block_top = largest(fold(jnp.maximum, s)) * TO_LOG2
            top = block_top if i == 0 else jnp.maximum(tops[...], block_top)
            p = jnp.exp2(s * TO_LOG2 - top[:, :1])
            if i == 0:
                totals[...] = fold(jnp.add, p)
                acc[...] = weigh(i, p)
            else:
                factor = jnp.exp2(tops[...] - top)
                totals[...] = totals[...] * factor + fold(jnp.add, p)
                acc[...] = scaled(acc[...], factor) + weigh(i, p)
            tops[...] = top
        finish(tops[...])

    @pl.when(live >= span)
    def _():
        one_pass(False)

    @pl.when((live > 0) & (live < span))
    def _():
        one_pass(True)

    @pl.when(live <= 0)
    def _():
        totals[...] = jnp.zeros(totals.shape, F32)
        acc[...] = jnp.zeros(acc.shape, F32)
        finish(jnp.full(tops.shape, MASKED, F32))


def attend(length, parts, cache, block=1024):
    group = parts[0].shape[0]
    rows, span = group * len(parts), cache.shape[1]
    return pl.pallas_call(
        functools.partial(attend_kernel, block=block),
        out_shape=[jax.ShapeDtypeStruct((group, PAYLOAD), BF16)] * len(parts),
        in_specs=[SMEM] + [VMEM] * (1 + len(parts)),
        out_specs=[VMEM] * len(parts),
        scratch_shapes=[
            pltpu.VMEM((rows, WIDTH), BF16),
            pltpu.VMEM((rows, 2 * block), F32),
            pltpu.VMEM((rows, 128), F32),
            pltpu.VMEM((rows, 128), F32),
            pltpu.VMEM((rows, LATENT), F32),
        ],
        compiler_params=pltpu.CompilerParams(vmem_limit_bytes=16 * 2**20),
        cost_estimate=pl.CostEstimate(
            flops=2 * rows * span * (WIDTH + LATENT), bytes_accessed=span * WIDTH * 2, transcendentals=rows * span
        ),
    )(length, cache, *parts)


def merge_kernel(*refs):
    parts, outs = refs[:RING], refs[RING:]
    columns, top, total = merge(parts)
    stats = pack_stats(top, total)
    rows = outs[0].shape[0]
    for at, out in enumerate(outs):
        here = slice(at * rows, (at + 1) * rows)
        for j, column in enumerate(columns):
            out[:, j * 128 : (j + 1) * 128] = column[here].astype(BF16)
        out[:, LATENT:] = stats[here]


def merge_groups(parts):
    rows, width = parts[0].shape
    return pl.pallas_call(
        merge_kernel,
        out_shape=[jax.ShapeDtypeStruct((rows // RING, width), BF16)] * RING,
        in_specs=[VMEM] * RING,
        out_specs=[VMEM] * RING,
        compiler_params=SMALL,
    )(*parts)


def pair_kernel(mine, other, out):
    core = lax.rem(lax.axis_index("roll"), CORES)
    out[core] = mine[...]
    out[1 - core] = other[...]


def pair(mine, other):
    return pl.pallas_call(
        pair_kernel,
        out_shape=jax.ShapeDtypeStruct((CORES,) + mine.shape, BF16),
        in_specs=[VMEM, VMEM],
        out_specs=VMEM,
        compiler_params=SMALL,
    )(mine, other)


def finish_kernel(a, b, c, d, w0, w1, w2, w3, out, context, weight):
    for owner, block in zip(y_owners(), (w0, w1, w2, w3)):
        for core in range(CORES):
            weight[:, pl.ds(pl.multiple_of((owner * CORES + core) * 64, 64), 64), :] = block[core]
    for j, column in enumerate(merge([a, b, c, d])[0]):
        context[:, j * 128 : (j + 1) * 128] = column.astype(BF16)
    frames, heads, _ = out.shape
    for h in range(heads):
        out[:, h, :] = jnp.dot(
            context[h * frames : (h + 1) * frames, :], weight[h], preferred_element_type=F32
        ).astype(BF16)


def finish(parts, weights, frames):
    _, heads, _, vhead = weights[0].shape
    return pl.pallas_call(
        finish_kernel,
        out_shape=jax.ShapeDtypeStruct((frames, heads, vhead), BF16),
        in_specs=[VMEM] * 8,
        out_specs=VMEM,
        scratch_shapes=[
            pltpu.VMEM((frames * heads, LATENT), BF16),
            pltpu.VMEM((heads, LATENT, vhead), BF16),
        ],
        compiler_params=SMALL,
    )(*parts, *weights)


def on_device(queries, latent_cache, lengths, key_weight, value_weight):
    frames = queries.shape[1]
    lengths = lengths.astype(jnp.int32)
    cache, block = latent_cache[0].T, jnp.swapaxes(key_weight, 1, 2)
    mine = queries[0]

    blocks = [y_shift(block, hops) for hops in (1, 2, 3)]
    other, value_other = core_swap(mine), core_swap(value_weight)
    cache, block, mine, value_mine = load(cache, block, mine, value_weight)
    own, others = absorb(mine, other, [block] + blocks)
    value_pair = pair(value_mine, value_other)
    local = own + core_swap(others)

    local, value_pair = lax.optimization_barrier((local, value_pair))
    near = stack([local] + [first_shift(local, hops) for hops in (1, 2, 3)])
    groups = [near] + [second_shift(near, hops) for hops in (1, 2, 3)]
    value_pairs = [value_pair] + [y_shift(value_pair, hops) for hops in (1, 2, 3)]

    away = attend(lengths, groups[1:], cache)
    groups, value_pairs = lax.optimization_barrier((groups, value_pairs))
    (zero,) = attend(lengths, groups[:1], cache)
    parts = [zero] + [second_shift(part, -hops) for hops, part in enumerate(away, 1)]

    near = merge_groups(parts)
    last = [near[0]] + [first_shift(near[hops], -hops) for hops in (1, 2, 3)]
    return finish(last, value_pairs, frames)[None]


def solution(mesh):
    placed = (
        P("roll", None, "seq", None),
        P("roll", "seq", None),
        P("roll"),
        P("seq", None, "roll"),
        P("seq", "roll", None),
    )
    return jax.shard_map(
        on_device,
        mesh=mesh,
        in_specs=placed,
        out_specs=P("roll", None, "seq", None),
        check_vma=False,
    )
```

```python
import functools

import jax
import jax.numpy as jnp
from jax import lax
from jax.experimental import pallas as pl
from jax.experimental.pallas import tpu as pltpu
from jax.sharding import PartitionSpec as P

NOPE = 128
ROPE = 64
LATENT = 512
WIDTH = LATENT + ROPE
PAYLOAD = LATENT + 128
RING = 4
CORES = 2

MASKED = -(2.0**100)
TO_LOG2 = (NOPE + ROPE) ** (-0.5) * 1.4426950408889634

VMEM = pl.BlockSpec(memory_space=pltpu.VMEM)
SMEM = pl.BlockSpec(memory_space=pltpu.SMEM)
SMALL = pltpu.CompilerParams(vmem_limit_bytes=4 * 2**20)
BF16 = jnp.bfloat16
F32 = jnp.float32


def exchange(value, move):
    pairs = []
    for y in range(RING):
        for core in range(CORES):
            for z in range(RING):
                for x in range(RING):
                    to_y, to_core, to_z, to_x = (at % size for at, size in zip(move(y, core, z, x), (RING, CORES, RING, RING)))
                    source = ((y * CORES + core) * RING + z) * RING + x
                    target = ((to_y * CORES + to_core) * RING + to_z) * RING + to_x
                    pairs.append((source, target))
    return lax.ppermute(value, ("roll", "seq"), pairs)


def core_swap(value):
    return exchange(value, lambda y, core, z, x: (y, core + 1, z, x))


def y_shift(value, hops):
    return exchange(value, lambda y, core, z, x: (y + hops, core, z, x))


def y_owners():
    y = lax.axis_index("roll") // CORES
    return [lax.rem(y + RING - hops, RING) for hops in range(RING)]


def first_shift(value, hops):
    return exchange(value, lambda y, core, z, x: (y, core, z + hops * (1 - core), x + hops * core))


def second_shift(value, hops):
    return exchange(value, lambda y, core, z, x: (y, core, z + hops * core, x + hops * (1 - core)))


def two_terms(value):
    high = value.astype(BF16).astype(F32)
    return high, (value - high).astype(BF16).astype(F32)


def pack_stats(top, total):
    lane = lax.broadcasted_iota(jnp.int32, top.shape, 1)
    packed = jnp.zeros(top.shape, F32)
    for at, term in enumerate(two_terms(top) + two_terms(total)):
        packed = jnp.where(lane == at, term, packed)
    return packed.astype(BF16)


def spread(stats, first):
    row = lax.broadcasted_iota(jnp.int32, (128, 128), 0)
    chosen = ((row == first) | (row == first + 1)).astype(F32).astype(BF16)
    return jnp.dot(stats, chosen, preferred_element_type=F32)


def merge(parts):
    tops = [spread(part[:, LATENT:], 0) for part in parts]
    totals = [spread(part[:, LATENT:], 2) for part in parts]
    top = functools.reduce(jnp.maximum, tops)
    weights = [jnp.exp2(t - top) * n for t, n in zip(tops, totals)]
    total = functools.reduce(jnp.add, weights)
    inverse = jnp.where(total > 0, 1.0 / total, 0.0)
    weights = [w * inverse for w in weights]
    columns = []
    for at in range(0, LATENT, 128):
        terms = [part[:, at : at + 128].astype(F32) * w for part, w in zip(parts, weights)]
        columns.append(functools.reduce(jnp.add, terms))
    return columns, top, total


def load_kernel(*refs):
    count = len(refs) // 2
    sems = refs[-1]
    copies = [pltpu.make_async_copy(refs[i], refs[count + i], sems.at[i]) for i in range(count)]
    for copy in copies:
        copy.start()
    for copy in copies:
        copy.wait()


def load(*arrays):
    return pl.pallas_call(
        load_kernel,
        out_shape=[jax.ShapeDtypeStruct(a.shape, a.dtype) for a in arrays],
        in_specs=[pl.BlockSpec(memory_space=pltpu.HBM)] * len(arrays),
        out_specs=[VMEM] * len(arrays),
        scratch_shapes=[pltpu.SemaphoreType.DMA((len(arrays),))],
        compiler_params=SMALL,
        cost_estimate=pl.CostEstimate(
            flops=0, bytes_accessed=2 * sum(a.size * 2 for a in arrays), transcendentals=0
        ),
    )(*[pltpu.with_memory_space_constraint(a, pltpu.HBM) for a in arrays])


def absorb_kernel(mine, other, kw0, kw1, kw2, kw3, out_mine, out_other, weights):
    core = lax.rem(lax.axis_index("roll"), CORES)
    frames, heads, _ = mine.shape
    weights[...] = jnp.zeros_like(weights)
    for owner, block in zip(y_owners(), (kw0, kw1, kw2, kw3)):
        chunk = owner * CORES + core
        weights[:, pl.ds(pl.multiple_of(chunk * 64, 64), 64), :] = block[...]
    absorbed = []
    for h in range(heads):
        rows = jnp.concatenate([mine[:, h, :NOPE], other[:, h, :NOPE]], axis=0)
        absorbed.append(
            lax.dot_general(rows, weights[h], (((1,), (1,)), ((), ())), preferred_element_type=F32)
        )
    out_mine[:, :LATENT] = jnp.concatenate([a[:frames] for a in absorbed], axis=0).astype(BF16)
    out_other[:, :LATENT] = jnp.concatenate([a[frames:] for a in absorbed], axis=0).astype(BF16)
    out_other[:, LATENT:] = jnp.zeros((heads * frames, ROPE), BF16)
    rope = [mine[:, h, NOPE:].astype(F32) for h in range(heads)]
    out_mine[:, LATENT:] = jnp.concatenate(rope, axis=0).astype(BF16)


def absorb(mine, other, blocks):
    frames, heads, _ = mine.shape
    shape = jax.ShapeDtypeStruct((heads * frames, WIDTH), BF16)
    return pl.pallas_call(
        absorb_kernel,
        out_shape=[shape, shape],
        in_specs=[VMEM] * 6,
        out_specs=[VMEM, VMEM],
        scratch_shapes=[pltpu.VMEM((heads, LATENT, NOPE), BF16)],
        compiler_params=SMALL,
    )(mine, other, *blocks)


def stack_kernel(*refs):
    parts, out = refs[:-1], refs[-1]
    rows = parts[0].shape[0]
    for at, part in enumerate(parts):
        out[at * rows : (at + 1) * rows, :] = part[...]


def stack(parts):
    rows, width = parts[0].shape
    return pl.pallas_call(
        stack_kernel,
        out_shape=jax.ShapeDtypeStruct((len(parts) * rows, width), BF16),
        in_specs=[VMEM] * len(parts),
        out_specs=VMEM,
        compiler_params=SMALL,
    )(*parts)


def fold(op, value):
    so_far = value[:, :128]
    for at in range(128, value.shape[1], 128):
        so_far = op(so_far, value[:, at : at + 128])
    return so_far


def attend_kernel(length, cache, *refs, block, first):
    turned, refs = (refs[-6], refs[:-6] + refs[-5:]) if first else (refs[0], refs[1:])
    count = (len(refs) - 5) // 2
    parts, outs = refs[:count], refs[count : 2 * count]
    query, scores, tops, totals, acc = refs[2 * count :]
    span = cache.shape[1]
    blocks = span // block
    live = jnp.clip(length[0] - lax.axis_index("seq") * span, 0, span)
    group = parts[0].shape[0]
    for at, part in enumerate(parts):
        query[at * group : (at + 1) * group, :] = part[...]

    def here(i):
        return pl.ds(i * block if isinstance(i, int) else pl.multiple_of(i * block, block), block)

    def score(i):
        return jnp.dot(query[...], cache[:, here(i)], preferred_element_type=F32)

    def weigh(i, p):
        if first:
            turned[here(i), :] = cache[:LATENT, here(i)].T
        return jnp.dot(p.astype(BF16), turned[here(i), :], preferred_element_type=F32)

    def largest(value):
        return jnp.broadcast_to(jnp.max(value, axis=1, keepdims=True), value.shape)

    def finish(top):
        total = jnp.broadcast_to(jnp.sum(totals[...], axis=1, keepdims=True), totals.shape)
        inverse = jnp.where(total > 0, 1.0 / total, 0.0)
        high, low = two_terms(top)
        sent = high + low
        stats = pack_stats(sent, total * jnp.exp2(top - sent))
        for at, out in enumerate(outs):
            rows = slice(at * group, (at + 1) * group)
            for column in range(0, LATENT, 128):
                lanes = slice(column, column + 128)
                out[:, lanes] = (acc[rows, lanes] * inverse[rows]).astype(BF16)
            out[:, LATENT:] = stats[rows]

    def scaled(value, factor):
        return jnp.concatenate([value[:, at : at + 128] * factor for at in range(0, LATENT, 128)], axis=1)

    def one_pass(masked):
        scores[:, here(0)] = score(0)
        for i in range(blocks):
            s = scores[:, here(i % 2)]
            if i + 1 < blocks:
                scores[:, here((i + 1) % 2)] = score(i + 1)
            if masked:
                column = lax.broadcasted_iota(jnp.int32, s.shape, 1)
                s = jnp.where(column < live - i * block, s, MASKED)
            block_top = largest(fold(jnp.maximum, s)) * TO_LOG2
            top = block_top if i == 0 else jnp.maximum(tops[...], block_top)
            p = jnp.exp2(s * TO_LOG2 - top[:, :1])
            if i == 0:
                totals[...] = fold(jnp.add, p)
                acc[...] = weigh(i, p)
            else:
                factor = jnp.exp2(tops[...] - top)
                totals[...] = totals[...] * factor + fold(jnp.add, p)
                acc[...] = scaled(acc[...], factor) + weigh(i, p)
            tops[...] = top
        finish(tops[...])

    @pl.when(live >= span)
    def _():
        one_pass(False)

    @pl.when((live > 0) & (live < span))
    def _():
        one_pass(True)

    @pl.when(live <= 0)
    def _():
        totals[...] = jnp.zeros(totals.shape, F32)
        acc[...] = jnp.zeros(acc.shape, F32)
        finish(jnp.full(tops.shape, MASKED, F32))


def attend(length, parts, cache, turned=None, block=1024):
    group = parts[0].shape[0]
    rows, span = group * len(parts), cache.shape[1]
    first = turned is None
    out_shape = [jax.ShapeDtypeStruct((group, PAYLOAD), BF16)] * len(parts)
    if first:
        out_shape.append(jax.ShapeDtypeStruct((span, LATENT), BF16))
    operands = [length, cache, *([] if first else [turned]), *parts]
    outs = pl.pallas_call(
        functools.partial(attend_kernel, block=block, first=first),
        out_shape=out_shape,
        in_specs=[SMEM] + [VMEM] * (len(operands) - 1),
        out_specs=[VMEM] * len(out_shape),
        scratch_shapes=[
            pltpu.VMEM((rows, WIDTH), BF16),
            pltpu.VMEM((rows, 2 * block), F32),
            pltpu.VMEM((rows, 128), F32),
            pltpu.VMEM((rows, 128), F32),
            pltpu.VMEM((rows, LATENT), F32),
        ],
        compiler_params=pltpu.CompilerParams(vmem_limit_bytes=16 * 2**20),
        cost_estimate=pl.CostEstimate(
            flops=2 * rows * span * (WIDTH + LATENT), bytes_accessed=span * WIDTH * 2, transcendentals=rows * span
        ),
    )(*operands)
    return (outs[:-1], outs[-1]) if first else (outs, turned)


def merge_kernel(*refs):
    parts, outs = refs[:RING], refs[RING:]
    columns, top, total = merge(parts)
    stats = pack_stats(top, total)
    rows = outs[0].shape[0]
    for at, out in enumerate(outs):
        here = slice(at * rows, (at + 1) * rows)
        for j, column in enumerate(columns):
            out[:, j * 128 : (j + 1) * 128] = column[here].astype(BF16)
        out[:, LATENT:] = stats[here]


def merge_groups(parts):
    rows, width = parts[0].shape
    return pl.pallas_call(
        merge_kernel,
        out_shape=[jax.ShapeDtypeStruct((rows // RING, width), BF16)] * RING,
        in_specs=[VMEM] * RING,
        out_specs=[VMEM] * RING,
        compiler_params=SMALL,
    )(*parts)


def pair_kernel(mine, other, out):
    core = lax.rem(lax.axis_index("roll"), CORES)
    out[core] = mine[...]
    out[1 - core] = other[...]


def pair(mine, other):
    return pl.pallas_call(
        pair_kernel,
        out_shape=jax.ShapeDtypeStruct((CORES,) + mine.shape, BF16),
        in_specs=[VMEM, VMEM],
        out_specs=VMEM,
        compiler_params=SMALL,
    )(mine, other)


def finish_kernel(a, b, c, d, w0, w1, w2, w3, out, context, weight):
    for owner, block in zip(y_owners(), (w0, w1, w2, w3)):
        for core in range(CORES):
            weight[:, pl.ds(pl.multiple_of((owner * CORES + core) * 64, 64), 64), :] = block[core]
    for j, column in enumerate(merge([a, b, c, d])[0]):
        context[:, j * 128 : (j + 1) * 128] = column.astype(BF16)
    frames, heads, _ = out.shape
    for h in range(heads):
        out[:, h, :] = jnp.dot(
            context[h * frames : (h + 1) * frames, :], weight[h], preferred_element_type=F32
        ).astype(BF16)


def finish(parts, weights, frames):
    _, heads, _, vhead = weights[0].shape
    return pl.pallas_call(
        finish_kernel,
        out_shape=jax.ShapeDtypeStruct((frames, heads, vhead), BF16),
        in_specs=[VMEM] * 8,
        out_specs=VMEM,
        scratch_shapes=[
            pltpu.VMEM((frames * heads, LATENT), BF16),
            pltpu.VMEM((heads, LATENT, vhead), BF16),
        ],
        compiler_params=SMALL,
    )(*parts, *weights)


def on_device(queries, latent_cache, lengths, key_weight, value_weight):
    frames = queries.shape[1]
    lengths = lengths.astype(jnp.int32)
    cache, block = latent_cache[0].T, jnp.swapaxes(key_weight, 1, 2)
    mine = queries[0]

    blocks = [y_shift(block, hops) for hops in (1, 2, 3)]
    other, value_other = core_swap(mine), core_swap(value_weight)
    cache, block, mine, value_mine = load(cache, block, mine, value_weight)
    own, others = absorb(mine, other, [block] + blocks)
    value_pair = pair(value_mine, value_other)
    local = own + core_swap(others)

    local, value_pair = lax.optimization_barrier((local, value_pair))
    near = stack([local] + [first_shift(local, hops) for hops in (1, 2, 3)])
    groups = [near] + [second_shift(near, hops) for hops in (1, 2, 3)]
    value_pairs = [value_pair] + [y_shift(value_pair, hops) for hops in (1, 2, 3)]

    (one, three), turned = attend(lengths, [groups[1], groups[3]], cache)
    groups, value_pairs = lax.optimization_barrier((groups, value_pairs))
    (two,), _ = attend(lengths, groups[2:3], cache, turned)
    (zero,), _ = attend(lengths, groups[:1], cache, turned)
    parts = [zero] + [second_shift(part, -hops) for hops, part in ((1, one), (2, two), (3, three))]

    near = merge_groups(parts)
    last = [near[0]] + [first_shift(near[hops], -hops) for hops in (1, 2, 3)]
    return finish(last, value_pairs, frames)[None]


def solution(mesh):
    placed = (
        P("roll", None, "seq", None),
        P("roll", "seq", None),
        P("roll"),
        P("seq", None, "roll"),
        P("seq", "roll", None),
    )
    return jax.shard_map(
        on_device,
        mesh=mesh,
        in_specs=placed,
        out_specs=P("roll", None, "seq", None),
        check_vma=False,
    )
```

```python
import functools

import jax
import jax.numpy as jnp
from jax import lax
from jax.experimental import pallas as pl
from jax.experimental.pallas import tpu as pltpu
from jax.sharding import PartitionSpec as P

NOPE = 128
ROPE = 64
LATENT = 512
WIDTH = LATENT + ROPE
PAYLOAD = LATENT + 128
RING = 4
CORES = 2

MASKED = -(2.0**100)
TO_LOG2 = (NOPE + ROPE) ** (-0.5) * 1.4426950408889634

VMEM = pl.BlockSpec(memory_space=pltpu.VMEM)
SMEM = pl.BlockSpec(memory_space=pltpu.SMEM)
SMALL = pltpu.CompilerParams(vmem_limit_bytes=4 * 2**20)
BF16 = jnp.bfloat16
F32 = jnp.float32


def exchange(value, move):
    pairs = []
    for y in range(RING):
        for core in range(CORES):
            for z in range(RING):
                for x in range(RING):
                    to_y, to_core, to_z, to_x = (at % size for at, size in zip(move(y, core, z, x), (RING, CORES, RING, RING)))
                    source = ((y * CORES + core) * RING + z) * RING + x
                    target = ((to_y * CORES + to_core) * RING + to_z) * RING + to_x
                    pairs.append((source, target))
    return lax.ppermute(value, ("roll", "seq"), pairs)


def core_swap(value):
    return exchange(value, lambda y, core, z, x: (y, core + 1, z, x))


def y_shift(value, hops):
    return exchange(value, lambda y, core, z, x: (y + hops, core, z, x))


def y_owners():
    y = lax.axis_index("roll") // CORES
    return [lax.rem(y + RING - hops, RING) for hops in range(RING)]


def first_shift(value, hops):
    return exchange(value, lambda y, core, z, x: (y, core, z + hops * (1 - core), x + hops * core))


def second_shift(value, hops):
    return exchange(value, lambda y, core, z, x: (y, core, z + hops * core, x + hops * (1 - core)))


def two_terms(value):
    high = value.astype(BF16).astype(F32)
    return high, (value - high).astype(BF16).astype(F32)


def pack_stats(top, total):
    lane = lax.broadcasted_iota(jnp.int32, top.shape, 1)
    packed = jnp.zeros(top.shape, F32)
    for at, term in enumerate(two_terms(top) + two_terms(total)):
        packed = jnp.where(lane == at, term, packed)
    return packed.astype(BF16)


def spread(stats, first):
    row = lax.broadcasted_iota(jnp.int32, (128, 128), 0)
    chosen = ((row == first) | (row == first + 1)).astype(F32).astype(BF16)
    return jnp.dot(stats, chosen, preferred_element_type=F32)


def merge(parts):
    tops = [spread(part[:, LATENT:], 0) for part in parts]
    totals = [spread(part[:, LATENT:], 2) for part in parts]
    top = functools.reduce(jnp.maximum, tops)
    weights = [jnp.exp2(t - top) * n for t, n in zip(tops, totals)]
    total = functools.reduce(jnp.add, weights)
    inverse = jnp.where(total > 0, 1.0 / total, 0.0)
    weights = [w * inverse for w in weights]
    columns = []
    for at in range(0, LATENT, 128):
        terms = [part[:, at : at + 128].astype(F32) * w for part, w in zip(parts, weights)]
        columns.append(functools.reduce(jnp.add, terms))
    return columns, top, total


def load_kernel(*refs):
    count = len(refs) // 2
    sems = refs[-1]
    copies = [pltpu.make_async_copy(refs[i], refs[count + i], sems.at[i]) for i in range(count)]
    for copy in copies:
        copy.start()
    for copy in copies:
        copy.wait()


def load(*arrays):
    return pl.pallas_call(
        load_kernel,
        out_shape=[jax.ShapeDtypeStruct(a.shape, a.dtype) for a in arrays],
        in_specs=[pl.BlockSpec(memory_space=pltpu.HBM)] * len(arrays),
        out_specs=[VMEM] * len(arrays),
        scratch_shapes=[pltpu.SemaphoreType.DMA((len(arrays),))],
        compiler_params=SMALL,
        cost_estimate=pl.CostEstimate(
            flops=0, bytes_accessed=2 * sum(a.size * 2 for a in arrays), transcendentals=0
        ),
    )(*[pltpu.with_memory_space_constraint(a, pltpu.HBM) for a in arrays])


def absorb_kernel(mine, other, kw0, kw1, kw2, kw3, out_mine, out_other, weights):
    core = lax.rem(lax.axis_index("roll"), CORES)
    frames, heads, _ = mine.shape
    weights[...] = jnp.zeros_like(weights)
    for owner, block in zip(y_owners(), (kw0, kw1, kw2, kw3)):
        chunk = owner * CORES + core
        weights[:, pl.ds(pl.multiple_of(chunk * 64, 64), 64), :] = block[...]
    absorbed = []
    for h in range(heads):
        rows = jnp.concatenate([mine[:, h, :NOPE], other[:, h, :NOPE]], axis=0)
        absorbed.append(
            lax.dot_general(rows, weights[h], (((1,), (1,)), ((), ())), preferred_element_type=F32)
        )
    out_mine[:, :LATENT] = jnp.concatenate([a[:frames] for a in absorbed], axis=0).astype(BF16)
    out_other[:, :LATENT] = jnp.concatenate([a[frames:] for a in absorbed], axis=0).astype(BF16)
    out_other[:, LATENT:] = jnp.zeros((heads * frames, ROPE), BF16)
    rope = [mine[:, h, NOPE:].astype(F32) for h in range(heads)]
    out_mine[:, LATENT:] = jnp.concatenate(rope, axis=0).astype(BF16)


def absorb(mine, other, blocks):
    frames, heads, _ = mine.shape
    shape = jax.ShapeDtypeStruct((heads * frames, WIDTH), BF16)
    return pl.pallas_call(
        absorb_kernel,
        out_shape=[shape, shape],
        in_specs=[VMEM] * 6,
        out_specs=[VMEM, VMEM],
        scratch_shapes=[pltpu.VMEM((heads, LATENT, NOPE), BF16)],
        compiler_params=SMALL,
    )(mine, other, *blocks)


def stack_kernel(*refs):
    parts, out = refs[:-1], refs[-1]
    rows = parts[0].shape[0]
    for at, part in enumerate(parts):
        out[at * rows : (at + 1) * rows, :] = part[...]


def stack(parts):
    rows, width = parts[0].shape
    return pl.pallas_call(
        stack_kernel,
        out_shape=jax.ShapeDtypeStruct((len(parts) * rows, width), BF16),
        in_specs=[VMEM] * len(parts),
        out_specs=VMEM,
        compiler_params=SMALL,
    )(*parts)


def fold(op, value):
    so_far = value[:, :128]
    for at in range(128, value.shape[1], 128):
        so_far = op(so_far, value[:, at : at + 128])
    return so_far


def attend_kernel(length, cache, *refs, block, first):
    turned, refs = (refs[-6], refs[:-6] + refs[-5:]) if first else (refs[0], refs[1:])
    count = (len(refs) - 5) // 2
    parts, outs = refs[:count], refs[count : 2 * count]
    query, scores, tops, totals, acc = refs[2 * count :]
    span = cache.shape[1]
    blocks = span // block
    live = jnp.clip(length[0] - lax.axis_index("seq") * span, 0, span)
    group = parts[0].shape[0]
    for at, part in enumerate(parts):
        query[at * group : (at + 1) * group, :] = part[...]

    def here(i):
        return pl.ds(i * block if isinstance(i, int) else pl.multiple_of(i * block, block), block)

    def score(i):
        return jnp.dot(query[...], cache[:, here(i)], preferred_element_type=F32)

    def weigh(i, p):
        if first:
            turned[here(i), :] = cache[:LATENT, here(i)].T
        return jnp.dot(p.astype(BF16), turned[here(i), :], preferred_element_type=F32)

    def largest(value):
        return jnp.broadcast_to(jnp.max(value, axis=1, keepdims=True), value.shape)

    def finish(top):
        total = jnp.broadcast_to(jnp.sum(totals[...], axis=1, keepdims=True), totals.shape)
        inverse = jnp.where(total > 0, 1.0 / total, 0.0)
        high, low = two_terms(top)
        sent = high + low
        stats = pack_stats(sent, total * jnp.exp2(top - sent))
        for at, out in enumerate(outs):
            rows = slice(at * group, (at + 1) * group)
            for column in range(0, LATENT, 128):
                lanes = slice(column, column + 128)
                out[:, lanes] = (acc[rows, lanes] * inverse[rows]).astype(BF16)
            out[:, LATENT:] = stats[rows]

    def scaled(value, factor):
        return jnp.concatenate([value[:, at : at + 128] * factor for at in range(0, LATENT, 128)], axis=1)

    def one_pass(masked):
        scores[:, here(0)] = score(0)
        for i in range(blocks):
            s = scores[:, here(i % 2)]
            if i + 1 < blocks:
                scores[:, here((i + 1) % 2)] = score(i + 1)
            if masked:
                column = lax.broadcasted_iota(jnp.int32, s.shape, 1)
                s = jnp.where(column < live - i * block, s, MASKED)
            block_top = largest(fold(jnp.maximum, s)) * TO_LOG2
            top = block_top if i == 0 else jnp.maximum(tops[...], block_top)
            p = jnp.exp2(s * TO_LOG2 - top[:, :1])
            if i == 0:
                totals[...] = fold(jnp.add, p)
                acc[...] = weigh(i, p)
            else:
                factor = jnp.exp2(tops[...] - top)
                totals[...] = totals[...] * factor + fold(jnp.add, p)
                acc[...] = scaled(acc[...], factor) + weigh(i, p)
            tops[...] = top
        finish(tops[...])

    @pl.when(live >= span)
    def _():
        one_pass(False)

    @pl.when((live > 0) & (live < span))
    def _():
        one_pass(True)

    @pl.when(live <= 0)
    def _():
        totals[...] = jnp.zeros(totals.shape, F32)
        acc[...] = jnp.zeros(acc.shape, F32)
        finish(jnp.full(tops.shape, MASKED, F32))


def attend(length, parts, cache, turned=None, block=2048):
    group = parts[0].shape[0]
    rows, span = group * len(parts), cache.shape[1]
    first = turned is None
    out_shape = [jax.ShapeDtypeStruct((group, PAYLOAD), BF16)] * len(parts)
    if first:
        out_shape.append(jax.ShapeDtypeStruct((span, LATENT), BF16))
    operands = [length, cache, *([] if first else [turned]), *parts]
    outs = pl.pallas_call(
        functools.partial(attend_kernel, block=block, first=first),
        out_shape=out_shape,
        in_specs=[SMEM] + [VMEM] * (len(operands) - 1),
        out_specs=[VMEM] * len(out_shape),
        scratch_shapes=[
            pltpu.VMEM((rows, WIDTH), BF16),
            pltpu.VMEM((rows, 2 * block), F32),
            pltpu.VMEM((rows, 128), F32),
            pltpu.VMEM((rows, 128), F32),
            pltpu.VMEM((rows, LATENT), F32),
        ],
        compiler_params=pltpu.CompilerParams(vmem_limit_bytes=16 * 2**20),
        cost_estimate=pl.CostEstimate(
            flops=2 * rows * span * (WIDTH + LATENT), bytes_accessed=span * WIDTH * 2, transcendentals=rows * span
        ),
    )(*operands)
    return (outs[:-1], outs[-1]) if first else (outs, turned)


def merge_kernel(*refs):
    parts, outs = refs[:RING], refs[RING:]
    columns, top, total = merge(parts)
    stats = pack_stats(top, total)
    rows = outs[0].shape[0]
    for at, out in enumerate(outs):
        here = slice(at * rows, (at + 1) * rows)
        for j, column in enumerate(columns):
            out[:, j * 128 : (j + 1) * 128] = column[here].astype(BF16)
        out[:, LATENT:] = stats[here]


def merge_groups(parts):
    rows, width = parts[0].shape
    return pl.pallas_call(
        merge_kernel,
        out_shape=[jax.ShapeDtypeStruct((rows // RING, width), BF16)] * RING,
        in_specs=[VMEM] * RING,
        out_specs=[VMEM] * RING,
        compiler_params=SMALL,
    )(*parts)


def pair_kernel(mine, other, out):
    core = lax.rem(lax.axis_index("roll"), CORES)
    out[core] = mine[...]
    out[1 - core] = other[...]


def pair(mine, other):
    return pl.pallas_call(
        pair_kernel,
        out_shape=jax.ShapeDtypeStruct((CORES,) + mine.shape, BF16),
        in_specs=[VMEM, VMEM],
        out_specs=VMEM,
        compiler_params=SMALL,
    )(mine, other)


def arrange_kernel(w0, w1, w2, w3, out):
    for owner, block in zip(y_owners(), (w0, w1, w2, w3)):
        for core in range(CORES):
            out[:, pl.ds(pl.multiple_of((owner * CORES + core) * 64, 64), 64), :] = block[core]


def arrange(blocks):
    _, heads, _, vhead = blocks[0].shape
    return pl.pallas_call(
        arrange_kernel,
        out_shape=jax.ShapeDtypeStruct((heads, LATENT, vhead), BF16),
        in_specs=[VMEM] * 4,
        out_specs=VMEM,
        compiler_params=SMALL,
    )(*blocks)


def finish_kernel(a, b, c, d, weight, out, context):
    for j, column in enumerate(merge([a, b, c, d])[0]):
        context[:, j * 128 : (j + 1) * 128] = column.astype(BF16)
    frames, heads, _ = out.shape
    for h in range(heads):
        out[:, h, :] = jnp.dot(
            context[h * frames : (h + 1) * frames, :], weight[h], preferred_element_type=F32
        ).astype(BF16)


def finish(parts, weight, frames):
    heads, _, vhead = weight.shape
    return pl.pallas_call(
        finish_kernel,
        out_shape=jax.ShapeDtypeStruct((frames, heads, vhead), BF16),
        in_specs=[VMEM] * 5,
        out_specs=VMEM,
        scratch_shapes=[pltpu.VMEM((frames * heads, LATENT), BF16)],
        compiler_params=SMALL,
    )(*parts, weight)


def on_device(queries, latent_cache, lengths, key_weight, value_weight):
    frames = queries.shape[1]
    lengths = lengths.astype(jnp.int32)
    cache, block = latent_cache[0].T, jnp.swapaxes(key_weight, 1, 2)
    mine = queries[0]

    blocks = [y_shift(block, hops) for hops in (1, 2, 3)]
    other, value_other = core_swap(mine), core_swap(value_weight)
    cache, block, mine, value_mine = load(cache, block, mine, value_weight)
    own, others = absorb(mine, other, [block] + blocks)
    value_pair = pair(value_mine, value_other)
    local = own + core_swap(others)

    local, value_pair = lax.optimization_barrier((local, value_pair))
    near = stack([local] + [first_shift(local, hops) for hops in (1, 2, 3)])
    groups = [near] + [second_shift(near, hops) for hops in (1, 2, 3)]
    value_pairs = [value_pair] + [y_shift(value_pair, hops) for hops in (1, 2, 3)]

    (one, two), turned = attend(lengths, [groups[1], groups[2]], cache)
    groups, value_pairs = lax.optimization_barrier((groups, value_pairs))
    (three,), _ = attend(lengths, groups[3:4], cache, turned)
    (zero,), _ = attend(lengths, groups[:1], cache, turned)
    parts = [zero] + [second_shift(part, -hops) for hops, part in ((1, one), (2, two), (3, three))]

    near = merge_groups(parts)
    last = [near[0]] + [first_shift(near[hops], -hops) for hops in (1, 2, 3)]
    return finish(last, arrange(value_pairs), frames)[None]


def solution(mesh):
    placed = (
        P("roll", None, "seq", None),
        P("roll", "seq", None),
        P("roll"),
        P("seq", None, "roll"),
        P("seq", "roll", None),
    )
    return jax.shard_map(
        on_device,
        mesh=mesh,
        in_specs=placed,
        out_specs=P("roll", None, "seq", None),
        check_vma=False,
    )
```
